32 devices in a mesh: dp: 4 (over z), ctx: 2 (over core), tensor: 4 (over y, x).
Axes of the slice: x: 2, y: 2, z: 4, core: 2. Of those that a mesh axis runs over, the one named last changes fastest.
Arguments:
- tokens: bfloat16 [4, 4096, 1024], P('dp', ('ctx', 'tensor')), may hold values from -6 to 6
- gain: bfloat16 [2, 1024], P(None, ('dp', 'ctx')), may hold values from 0.5 to 1.5
- w_z: bfloat16 [2, 1024, 2048], P(None, ('dp', 'ctx'), 'tensor'), may hold values from -0.1875 to 0.1875
- w_x: bfloat16 [2, 1024, 2048], P(None, ('dp', 'ctx'), 'tensor'), may hold values from -0.1875 to 0.1875
- w_bc: bfloat16 [2, 1024, 256], P(None, ('dp', 'ctx')), may hold values from -0.1875 to 0.1875
- w_dt: bfloat16 [2, 1024, 32], P(None, ('dp', 'ctx')), may hold values from -0.1875 to 0.1875
- conv_w: bfloat16 [2, 4, 2304], P(None, None, ('dp', 'ctx')), may hold values from -3 to 3
- conv_b: bfloat16 [2, 2304], P(None, ('dp', 'ctx')), may hold values from -0.5 to 0.5
- dt_bias: bfloat16 [2, 32], P(None, ('dp', 'ctx')), may hold values from -6 to -2
- a_log: bfloat16 [2, 32], P(None, ('dp', 'ctx')), may hold values from 0 to 2.5
- d_skip: bfloat16 [2, 32], P(None, ('dp', 'ctx')), may hold values from 0.5 to 1.5
- norm_w: bfloat16 [2, 2048], P(None, ('dp', 'ctx')), may hold values from 0.5 to 1.5
- w_out: bfloat16 [2, 2048, 1024], P(None, 'tensor', ('dp', 'ctx')), may hold values from -0.125 to 0.125
- cotangent: bfloat16 [4, 4096, 1024], P('dp', ('ctx', 'tensor')), may hold values from -6 to 6
Outputs:
- outputs: bfloat16 [4, 4096, 1024], P('dp', ('ctx', 'tensor'))
- grad_tokens: float32 [4, 4096, 1024], P('dp', ('ctx', 'tensor'))
- grad_gain: float32 [2, 1024], P(None, ('dp', 'ctx'))
- grad_w_z: float32 [2, 1024, 2048], P(None, ('dp', 'ctx'), 'tensor')
- grad_w_x: float32 [2, 1024, 2048], P(None, ('dp', 'ctx'), 'tensor')
- grad_w_bc: float32 [2, 1024, 256], P(None, ('dp', 'ctx'))
- grad_w_dt: float32 [2, 1024, 32], P(None, ('dp', 'ctx'))
- grad_conv_w: float32 [2, 4, 2304], P(None, None, ('dp', 'ctx'))
- grad_conv_b: float32 [2, 2304], P(None, ('dp', 'ctx'))
- grad_dt_bias: float32 [2, 32], P(None, ('dp', 'ctx'))
- grad_a_log: float32 [2, 32], P(None, ('dp', 'ctx'))
- grad_d_skip: float32 [2, 32], P(None, ('dp', 'ctx'))
- grad_norm_w: float32 [2, 2048], P(None, ('dp', 'ctx'))
- grad_w_out: float32 [2, 2048, 1024], P(None, 'tensor', ('dp', 'ctx'))
The draws below stay inside these ranges and needn't reach their ends.
All inputs are finite; a program needn't handle non-finite values.
Results may differ from the reference program's by a relative error of at most 0.03.
Values may be sent and summed in bfloat16 or wider, within the bound.
A program may use at most 256 MiB of HBM per device.

```python
import jax
import jax.numpy as jnp
from jax import lax

D = 1024
NH = 32
HEADDIM = 64
NSTATE = 128
KCONV = 4
SPAN = 256
LAYERS = 2
INNER = 2048
CH = 2304
LEN = 4096
SEQS = 4


def levels(key, extent, cuts, smallest, top_value):
    def one(dim, shards_of):
        heights = jax.random.uniform(jax.random.fold_in(jax.random.fold_in(key, 6), dim), (shards_of,), jnp.float32, smallest / len(cuts), top_value / len(cuts))
        return jnp.repeat(jnp.exp(heights), extent[dim] // shards_of).reshape((-1,) + (1,) * (len(extent) - dim - 1))

    level = one(*cuts[0])
    for cut in cuts[1:]:
        level = level * one(*cut)
    return level


def noise(rng, extent, width, bound, shards=(), kind=jnp.bfloat16):
    values = width * jax.random.normal(rng, extent, jnp.float32)
    if shards:
        values = values * levels(rng, extent, shards, -0.22, 0.18)
    return jnp.clip(values, -bound, bound).astype(kind)


def setup_inputs(seed: int = 0) -> dict:
    key_of = jax.random.split(jax.random.key(seed), 15)
    return {
        "tokens": noise(key_of[0], (SEQS, LEN, D), 1.0, 6.0, ((0, 4), (1, 8))),
        "gain": jnp.clip(1.0 + 0.1 * jax.random.normal(key_of[1], (LAYERS, D), jnp.float32), 0.5, 1.5).astype(jnp.bfloat16),
        "w_z": noise(key_of[2], (LAYERS, D, INNER), D ** -0.5, 0.1875, ((1, 8), (2, 4))),
        "w_x": noise(key_of[3], (LAYERS, D, INNER), D ** -0.5, 0.1875, ((1, 8), (2, 4))),
        "w_bc": noise(key_of[4], (LAYERS, D, 2 * NSTATE), D ** -0.5, 0.1875, ((1, 8),)),
        "w_dt": noise(key_of[5], (LAYERS, D, NH), D ** -0.5, 0.1875, ((1, 8),)),
        "conv_w": noise(key_of[6], (LAYERS, KCONV, CH), KCONV ** -0.5, 3.0, ((2, 8),)),
        "conv_b": jnp.clip(jax.random.uniform(key_of[7], (LAYERS, CH), jnp.float32, -0.5, 0.5) * levels(key_of[7], (LAYERS, CH), ((1, 8),), -0.4, 0.0), -0.5, 0.5).astype(jnp.bfloat16),
        "dt_bias": jnp.clip(-6.0 + 4.0 * jax.random.uniform(key_of[8], (LAYERS, NH), jnp.float32) ** levels(key_of[8], (LAYERS, NH), ((1, 8),), -0.2, 0.2), -6.0, -2.0).astype(jnp.bfloat16),
        "a_log": jnp.clip(2.5 * jax.random.uniform(key_of[9], (LAYERS, NH), jnp.float32) ** levels(key_of[9], (LAYERS, NH), ((1, 8),), -0.2, 0.2), 0.0, 2.5).astype(jnp.bfloat16),
        "d_skip": jnp.clip(0.5 + 1.0 * jax.random.uniform(key_of[10], (LAYERS, NH), jnp.float32) ** levels(key_of[10], (LAYERS, NH), ((1, 8),), -0.2, 0.2), 0.5, 1.5).astype(jnp.bfloat16),
        "norm_w": jnp.clip(1.0 + 0.1 * jax.random.normal(key_of[11], (LAYERS, INNER), jnp.float32), 0.5, 1.5).astype(jnp.bfloat16),
        "w_out": noise(key_of[12], (LAYERS, INNER, D), INNER ** -0.5, 0.125, ((1, 4), (2, 8))),
        "cotangent": noise(key_of[13], (SEQS, LEN, D), 1.0, 6.0, ((0, 4), (1, 8))),
    }


EPS = 1e-05
HIGH = lax.Precision.HIGHEST

@jax.custom_vjp
def low(v):
    return lax.optimization_barrier(v.astype(jnp.bfloat16)).astype(jnp.float32)

@jax.custom_vjp
def low_back(v):
    return v

def low_keep(v):
    return (low(v), None)

def low_pass(kept, grad):
    return (grad,)

def back_keep(v):
    return (v, None)

def back_low(kept, grad):
    return (low(grad),)
low.defvjp(low_keep, low_pass)
low_back.defvjp(back_keep, back_low)

def matmul(left, right):
    return jnp.dot(left, right, precision=HIGH, preferred_element_type=jnp.float32)

def ssd_block(state_in, inputs):
    head_x, proj_b, proj_c, delta_t, log_decay = inputs
    running = jnp.cumsum(log_decay, axis=0)
    positions = jnp.arange(head_x.shape[0])
    causal = (positions[:, None] >= positions[None, :])[:, :, None]
    spread = running[:, None, :] - running[None, :, :]
    kernel = jnp.where(causal, jnp.exp(jnp.where(causal, spread, 0.0)), 0.0)
    scores = matmul(proj_c, proj_b.T)
    mixing = scores[:, :, None] * kernel * delta_t[None, :, :]
    inside = jnp.einsum('tsh,shp->thp', mixing, head_x, precision=HIGH)
    carried = jnp.einsum('tn,hpn->thp', proj_c, state_in, precision=HIGH) * jnp.exp(running)[:, :, None]
    tail_weight = jnp.exp(running[-1][None, :] - running) * delta_t
    update = jnp.einsum('sh,sn,shp->hpn', tail_weight, proj_b, head_x, precision=HIGH)
    new_state = state_in * jnp.exp(running[-1])[:, None, None] + update
    return (new_state, inside + carried)

def scan_blocks(head_x, proj_b, proj_c, delta_t, log_decay, state_in):
    token_count = head_x.shape[0]
    block_count = token_count // SPAN
    pieces = (head_x.reshape(block_count, SPAN, head_x.shape[1], head_x.shape[2]), proj_b.reshape(block_count, SPAN, proj_b.shape[1]), proj_c.reshape(block_count, SPAN, proj_c.shape[1]), delta_t.reshape(block_count, SPAN, delta_t.shape[1]), log_decay.reshape(block_count, SPAN, log_decay.shape[1]))
    final_state, outputs = lax.scan(jax.checkpoint(ssd_block), state_in, pieces)
    return (final_state, outputs.reshape(head_x.shape))

def mixer_layer(residual, params):
    gain, w_z, w_x, w_bc, w_dt, conv_w, conv_b, dt_bias, a_log, d_skip, norm_w, w_out = params
    length = residual.shape[0]
    inv_rms = lax.rsqrt(lax.optimization_barrier(jnp.mean(residual * residual, axis=-1, keepdims=True)) + EPS)
    normed = low(residual * inv_rms * gain)
    proj_all = low_back(matmul(normed, jnp.concatenate([w_z, w_x, w_bc], axis=1)))
    gate_part = proj_all[:, :INNER]
    dt_raw = low_back(matmul(normed, w_dt))
    conv_in = low(proj_all[:, INNER:])
    padded = jnp.concatenate([jnp.zeros((KCONV - 1, conv_in.shape[1]), jnp.float32), conv_in], axis=0)
    conv_out = conv_b + sum((conv_w[offset] * padded[offset:offset + length] for offset in range(KCONV)))
    activated = low(jax.nn.silu(conv_out))
    head_x = activated[:, :INNER].reshape(length, NH, HEADDIM)
    proj_b = activated[:, INNER:INNER + NSTATE]
    proj_c = activated[:, INNER + NSTATE:]
    delta_t = jax.nn.softplus(dt_raw + dt_bias)
    log_decay = -jnp.exp(a_log) * delta_t
    zero_state = jnp.zeros((NH, HEADDIM, NSTATE), jnp.float32)
    final_state, scanned = scan_blocks(head_x, proj_b, proj_c, delta_t, log_decay, zero_state)
    scanned = scanned + d_skip[None, :, None] * head_x
    gated_y = scanned.reshape(length, INNER) * jax.nn.silu(gate_part)
    norm_scale = lax.rsqrt(lax.optimization_barrier(jnp.mean(gated_y * gated_y, axis=-1, keepdims=True)) + EPS)
    branch = low(gated_y * norm_w)
    partial_out = low_back(matmul(branch, w_out))
    return residual + norm_scale * partial_out

def reference(tokens, gain, w_z, w_x, w_bc, w_dt, conv_w, conv_b, dt_bias, a_log, d_skip, norm_w, w_out, cotangent):
    params = tuple((weight.astype(jnp.float32) for weight in (gain, w_z, w_x, w_bc, w_dt, conv_w, conv_b, dt_bias, a_log, d_skip, norm_w, w_out)))

    def forward(inputs, weights):

        def one_sequence(sequence):
            hidden = sequence
            for layer_index in range(LAYERS):
                hidden = mixer_layer(hidden, tuple((weight[layer_index] for weight in weights)))
            return hidden
        return lax.map(one_sequence, inputs)
    result, pullback = jax.vjp(forward, tokens.astype(jnp.float32), params)
    grad_in, grad_params = pullback(cotangent.astype(jnp.float32))
    return (result.astype(jnp.bfloat16), grad_in, grad_params[0], grad_params[1], grad_params[2], grad_params[3], grad_params[4], grad_params[5], grad_params[6], grad_params[7], grad_params[8], grad_params[9], grad_params[10], grad_params[11])
```

```python
import jax
import jax.numpy as jnp
from jax import lax
from jax.experimental import pallas as pl
from jax.experimental.pallas import tpu as pltpu
from jax.sharding import PartitionSpec as P

NH = 32
HEADDIM = 64
NSTATE = 128
KCONV = 4
SPAN = 256
LAYERS = 2
INNER = 2048
LANES = 128
SMALL_ROWS = 16

EPS = 1e-05
HIGH = lax.Precision.HIGHEST
BF = jnp.bfloat16
F32 = jnp.float32


def dot(left, right, lc=1, rc=0):
    return lax.dot_general(left, right, (((lc,), (rc,)), ((), ())), preferred_element_type=F32)


def exact(left, right):
    return jnp.dot(left, right, precision=HIGH, preferred_element_type=F32)


def silu_grad(values):
    sigmoid_v = jax.nn.sigmoid(values)
    return sigmoid_v * (1.0 + values * (1.0 - sigmoid_v))


def causal_mask(size):
    rows = lax.broadcasted_iota(jnp.int32, (size, size), 0)
    cols = lax.broadcasted_iota(jnp.int32, (size, size), 1)
    return rows >= cols


def scan_fwd_kernel(b_ref, c_ref, xd_ref, xw_ref, e_ref, a_ref, at_ref, el_ref, y_ref, s_ref, f_ref, state):
    @pl.when(pl.program_id(0) == 0)
    def _():
        state[...] = jnp.zeros_like(state)

    heads = a_ref.shape[1]
    b, c = b_ref[...], c_ref[...]
    held = state[...]
    s_ref[0] = held
    scores = jnp.where(causal_mask(b.shape[0]), dot(c, b, 1, 1), 0.0)
    carried = e_ref[...] * dot(c, held.astype(BF))
    for h in range(heads):
        at = slice(h * HEADDIM, (h + 1) * HEADDIM)
        spread = jnp.minimum(a_ref[:, h : h + 1] - at_ref[0, h : h + 1, :], 0.0)
        mixing = (scores * jnp.exp(spread)).astype(BF)
        y_ref[:, at] = dot(mixing, xd_ref[:, at]) + carried[:, at]
    new = el_ref[0] * held + dot(b, xw_ref[...], 0, 0)
    state[...] = new
    f_ref[...] = new


def scan_bwd_kernel(b_ref, c_ref, xd_ref, xw_ref, dy_ref, z_ref, a_ref, at_ref, el_ref, s_ref, df_ref,
                    dx_ref, v_ref, db_ref, dc_ref, r_ref, state):
    @pl.when(pl.program_id(0) == 0)
    def _():
        state[...] = df_ref[...]

    heads = a_ref.shape[1]
    b, c, xw, z = b_ref[...], c_ref[...], xw_ref[...], z_ref[...]
    held = state[...]
    low = held.astype(BF)
    entered = s_ref[0]
    mask = causal_mask(b.shape[0])
    scores = jnp.where(mask, dot(c, b, 1, 1), 0.0)
    v_ref[...] = dot(b, low)
    r_ref[0] = el_ref[0] * jnp.sum(held * entered, axis=0, keepdims=True)
    total = jnp.zeros(scores.shape, F32)
    for h in range(heads):
        at = slice(h * HEADDIM, (h + 1) * HEADDIM)
        decays = jnp.exp(jnp.minimum(a_ref[:, h : h + 1] - at_ref[0, h : h + 1, :], 0.0))
        mixing = (scores * decays).astype(BF)
        dy = dy_ref[:, at]
        dx_ref[:, at] = dot(mixing, dy, 0, 0)
        total = total + decays * dot(dy, xd_ref[:, at], 1, 1)
    total = jnp.where(mask, total, 0.0).astype(BF)
    dc_ref[...] = dot(total, b) + dot(z, entered.astype(BF), 1, 1)
    db_ref[...] = dot(total, c, 0, 0) + dot(xw, low, 1, 1)
    state[...] = el_ref[0] * held + dot(c, z, 0, 0)


def rows_of(width, order):
    return pl.BlockSpec((SPAN, width), lambda k: (order(k), 0))


def one_of(rows, width, order):
    return pl.BlockSpec((1, rows, width), lambda k: (order(k), 0, 0))


PARAMS = pltpu.CompilerParams(vmem_limit_bytes=48 * 1024 * 1024)


def scan_fwd(b, c, xd, xw, e, a, at, el):
    length, wide = xd.shape
    heads, count = a.shape[1], length // SPAN
    order = lambda k: k
    return pl.pallas_call(
        scan_fwd_kernel,
        grid=(count,),
        in_specs=[
            rows_of(NSTATE, order), rows_of(NSTATE, order), rows_of(wide, order), rows_of(wide, order),
            rows_of(wide, order), rows_of(heads, order), one_of(heads, SPAN, order), one_of(1, wide, order),
        ],
        out_specs=[
            rows_of(wide, order), one_of(NSTATE, wide, order),
            pl.BlockSpec((NSTATE, wide), lambda k: (0, 0)),
        ],
        out_shape=[
            jax.ShapeDtypeStruct((length, wide), F32),
            jax.ShapeDtypeStruct((count, NSTATE, wide), F32),
            jax.ShapeDtypeStruct((NSTATE, wide), F32),
        ],
        scratch_shapes=[pltpu.VMEM((NSTATE, wide), F32)],
        compiler_params=PARAMS,
    )(b, c, xd, xw, e, a, at, el)


def scan_bwd(b, c, xd, xw, dy, z, a, at, el, s, df):
    length, wide = xd.shape
    heads, count = a.shape[1], length // SPAN
    order = lambda k: count - 1 - k
    return pl.pallas_call(
        scan_bwd_kernel,
        grid=(count,),
        in_specs=[
            rows_of(NSTATE, order), rows_of(NSTATE, order), rows_of(wide, order), rows_of(wide, order),
            rows_of(wide, order), rows_of(wide, order), rows_of(heads, order), one_of(heads, SPAN, order),
            one_of(1, wide, order), one_of(NSTATE, wide, order),
            pl.BlockSpec((NSTATE, wide), lambda k: (0, 0)),
        ],
        out_specs=[
            rows_of(wide, order), rows_of(wide, order), rows_of(NSTATE, order), rows_of(NSTATE, order),
            one_of(1, wide, order),
        ],
        out_shape=[
            jax.ShapeDtypeStruct((length, wide), F32),
            jax.ShapeDtypeStruct((length, wide), F32),
            jax.ShapeDtypeStruct((length, NSTATE), F32),
            jax.ShapeDtypeStruct((length, NSTATE), F32),
            jax.ShapeDtypeStruct((count, 1, wide), F32),
        ],
        scratch_shapes=[pltpu.VMEM((NSTATE, wide), F32)],
        compiler_params=PARAMS,
    )(b, c, xd, xw, dy, z, a, at, el, s, df)


def pack_small(pieces, width):
    flat = jnp.concatenate([piece.reshape(-1) for piece in pieces])
    return jnp.pad(flat, (0, SMALL_ROWS * width - flat.shape[0])).reshape(SMALL_ROWS, width)


def fetch_layer(stack, layer):
    gain, w_z, w_x, w_bc, w_dt, conv_w, conv_b, dt_bias, a_log, d_skip, norm_w, w_out = (
        weight[layer] for weight in stack
    )
    rows, inner = w_z.shape
    main = jnp.concatenate([w_z, w_x, w_bc, w_dt, w_out.T], axis=1)
    width = main.shape[1]
    small = (conv_w, conv_b, norm_w, gain, dt_bias, a_log, d_skip)
    full = lax.all_gather(jnp.concatenate([main, pack_small(small, width)], axis=0), ("dp", "ctx"), axis=0)
    peers = full.shape[0]
    wide = full[:, :rows].reshape(peers * rows, width)
    w_main = wide[:, : 2 * inner + 2 * NSTATE]
    at = 2 * inner + 2 * NSTATE
    w_dt_all = wide[:, at : at + NH]
    w_out_t = wide[:, at + NH :]
    flat = full[:, rows:].reshape(peers, -1)
    out, at = [], 0
    for piece in small:
        part = flat[:, at : at + piece.size].reshape((peers,) + piece.shape)
        out.append(jnp.moveaxis(part, 0, -2).reshape(piece.shape[:-1] + (-1,)).astype(F32))
        at += piece.size
    return (w_main, w_dt_all, w_out_t) + tuple(out)


def reduce_layer(parts, peers):
    main, small = parts
    rows = main.shape[0] // peers
    width = main.shape[1]
    flat = jnp.concatenate(
        [
            jnp.moveaxis(p.reshape(p.shape[:-1] + (peers, p.shape[-1] // peers)), -2, 0).reshape(peers, -1)
            for p in small
        ],
        axis=1,
    )
    flat = jnp.pad(flat, ((0, 0), (0, SMALL_ROWS * width - flat.shape[1]))).reshape(peers, SMALL_ROWS, width)
    whole = jnp.concatenate([main.reshape(peers, rows, width), flat.astype(BF)], axis=1)
    return lax.psum_scatter(whole, ("dp", "ctx"), scatter_dimension=0, tiled=False)


def own(vector, start, count):
    return lax.dynamic_slice_in_dim(vector, start, count, vector.ndim - 1)


def place(width, piece, start):
    return lax.dynamic_update_slice_in_dim(
        jnp.zeros(piece.shape[:-1] + (width,), F32), piece, start, piece.ndim - 1
    )


def split_cols(column):
    high = column.astype(BF)
    return high, (column - high.astype(F32)).astype(BF)


def layer_forward(residual, gathered, tensor_at, inner_loc, heads_loc, ctx_at):
    w_main, w_dt, w_out_t, conv_w, conv_b, norm_w, gain, dt_bias, a_log, d_skip = gathered
    head_start = tensor_at * heads_loc
    chan_start = tensor_at * inner_loc
    inv_rms = lax.rsqrt(jnp.mean(residual * residual, axis=-1, keepdims=True) + EPS)
    normed = (residual * inv_rms * gain).astype(BF)
    rows_all = lax.all_gather(normed, "tensor", axis=0, tiled=True)
    length = rows_all.shape[0]
    gate = dot(rows_all, w_main[:, :inner_loc])
    conv_in = dot(rows_all, w_main[:, inner_loc:]).astype(BF)
    w_dt_own = own(w_dt, head_start, heads_loc)
    dt_raw = dot(rows_all, w_dt_own)
    edge = lax.ppermute(conv_in[length - (KCONV - 1) :], "ctx", [(0, 1)])
    conv_w_own = jnp.concatenate([own(conv_w, chan_start, inner_loc), conv_w[:, INNER:]], axis=1)
    conv_b_own = jnp.concatenate([own(conv_b, chan_start, inner_loc), conv_b[INNER:]], axis=0)
    padded = jnp.concatenate([edge, conv_in], axis=0)
    conv_out = conv_b_own + sum(
        conv_w_own[k] * padded[k : k + length].astype(F32) for k in range(KCONV)
    )
    activated = jax.nn.silu(conv_out).astype(BF)
    x = activated[:, :inner_loc]
    b = activated[:, inner_loc : inner_loc + NSTATE]
    c = activated[:, inner_loc + NSTATE :]
    dt_pre = dt_raw + own(dt_bias, head_start, heads_loc)
    delta = jax.nn.softplus(dt_pre)
    rate = -jnp.exp(own(a_log, head_start, heads_loc))
    log_decay = rate * delta
    count = length // SPAN
    spread = jnp.repeat(jnp.eye(heads_loc, dtype=F32), HEADDIM, axis=1)
    lower = causal_mask(SPAN).astype(F32)
    a3 = jnp.einsum("ts,ksh->kth", lower, log_decay.reshape(count, SPAN, heads_loc), precision=HIGH)
    a = a3.reshape(length, heads_loc)
    at = jnp.swapaxes(a3, 1, 2)
    last = a3[:, -1]
    tail = jnp.exp(last[:, None] - a3).reshape(length, heads_loc)
    e_wide = exact(jnp.exp(a), spread)
    delta_wide = exact(delta, spread)
    tail_wide = exact(tail, spread)
    xf = x.astype(F32)
    xd = (xf * delta_wide).astype(BF)
    xw = (xf * (delta_wide * tail_wide)).astype(BF)
    el = exact(jnp.exp(last), spread)[:, None]
    local_y, local_s, final_s = scan_fwd(b, c, xd, xw, e_wide, a, at, el)
    strict = 1.0 - causal_mask(count).astype(F32).T
    before = exact(strict, last)
    first = lax.ppermute(final_s.astype(BF), "ctx", [(0, 1)])
    before_wide = exact(jnp.exp(before), spread)
    e_total = (e_wide.reshape(count, SPAN, -1) * before_wide[:, None]).reshape(length, inner_loc)
    entered = local_s + before_wide[:, None] * first.astype(F32)[None]
    y = local_y + e_total * dot(c, first)
    skip_wide = exact(own(d_skip, head_start, heads_loc)[None], spread)
    scanned = y + skip_wide * xf
    gated = scanned * jax.nn.silu(gate)
    squares = jnp.sum(gated * gated, axis=-1, keepdims=True)
    norm_own = own(norm_w, chan_start, inner_loc)
    branch = (gated * norm_own).astype(BF)
    partial = dot(branch, w_out_t, 1, 1).astype(BF)
    packed = jnp.concatenate(
        [partial, jnp.broadcast_to(squares.astype(BF), (length, LANES))], axis=1
    )
    summed = lax.psum_scatter(packed, "tensor", scatter_dimension=0, tiled=True).astype(F32)
    out_own = summed[:, : partial.shape[1]]
    q = lax.rsqrt(summed[:, partial.shape[1] : partial.shape[1] + 1] / INNER + EPS)
    saved = (
        residual, inv_rms, rows_all, gate, conv_w_own, padded, conv_out, b, c, x, xd, xw, e_wide, e_total,
        delta_wide, tail_wide, a, at, el, entered, y, scanned, gated, branch, out_own, q, w_dt_own,
        skip_wide, norm_own, dt_pre, delta, rate, spread, lower,
    )
    return residual + q * out_own, saved


def layer_backward(grad_own, gathered, saved, tensor_at, inner_loc, heads_loc, ctx_at):
    w_main, w_dt, w_out_t, conv_w, conv_b, norm_w, gain, dt_bias, a_log, d_skip = gathered
    (
        residual, inv_rms, rows_all, gate, conv_w_own, padded, conv_out, b, c, x, xd, xw, e_wide, e_total,
        delta_wide, tail_wide, a, at, el, entered, y, scanned, gated, branch, out_own, q, w_dt_own,
        skip_wide, norm_own, dt_pre, delta, rate, spread, lower,
    ) = saved
    head_start = tensor_at * heads_loc
    chan_start = tensor_at * inner_loc
    length = rows_all.shape[0]
    features = residual.shape[1]
    count = length // SPAN
    dq = jnp.sum(grad_own * out_own, axis=-1, keepdims=True)
    high, rest = split_cols(dq * q * q * q / INNER)
    packed = jnp.concatenate(
        [
            (q * grad_own).astype(BF),
            jnp.broadcast_to(high, (high.shape[0], LANES // 2)),
            jnp.broadcast_to(rest, (high.shape[0], LANES // 2)),
        ],
        axis=1,
    )
    arrived = lax.all_gather(packed, "tensor", axis=0, tiled=True)
    grad_rows = arrived[:, :features]
    scale = (
        arrived[:, features : features + 1].astype(F32)
        + arrived[:, features + LANES // 2 : features + LANES // 2 + 1].astype(F32)
    )
    grad_wout_t = dot(grad_rows, branch, 0, 0)
    grad_branch = dot(grad_rows, w_out_t)
    grad_normw = jnp.sum(grad_branch * gated, axis=0)
    grad_gated = grad_branch * norm_own - scale * gated
    dy = grad_gated * jax.nn.silu(gate)
    grad_gate = grad_gated * scanned * silu_grad(gate)
    xf = x.astype(F32)
    heads = lambda wide: exact(wide, spread.T)
    grad_skip = heads(jnp.sum(dy * xf, axis=0, keepdims=True))[0]
    dy_low = dy.astype(BF)
    z = (e_wide * dy).astype(BF)
    first_grad = dot(c, (e_total * dy).astype(BF), 0, 0)
    final_grad = lax.ppermute(first_grad.astype(BF), "ctx", [(1, 0)]).astype(F32)
    dxp, v, db, dc, carry = scan_bwd(b, c, xd, xw, dy_low, z, a, at, el, entered, final_grad)
    pulled = dxp + tail_wide * v
    grad_x = delta_wide * pulled + skip_wide * dy
    grad_dt = heads(xf * pulled)
    moved = xw.astype(F32) * v
    grad_a = heads(dy_low.astype(F32) * y - xd.astype(F32) * dxp - moved).reshape(count, SPAN, heads_loc)
    ends = heads(carry[:, 0] + jnp.sum(moved.reshape(count, SPAN, inner_loc), axis=1))
    grad_decay = (
        jnp.einsum("ts,kth->ksh", lower, grad_a, precision=HIGH) + ends[:, None]
    ).reshape(length, heads_loc)
    grad_delta = grad_dt + grad_decay * rate
    grad_alog = jnp.sum(grad_decay * delta, axis=0) * rate
    grad_pre = grad_delta * jax.nn.sigmoid(dt_pre)
    grad_dtbias = jnp.sum(grad_pre, axis=0)
    grad_pre_low = grad_pre.astype(BF)
    grad_conv = jnp.concatenate([grad_x, db, dc], axis=1) * silu_grad(conv_out)
    grad_convb = jnp.sum(grad_conv, axis=0)
    grad_convw = jnp.stack(
        [jnp.sum(grad_conv * padded[k : k + length].astype(F32), axis=0) for k in range(KCONV)]
    )
    head_rows = lax.ppermute(grad_conv[: KCONV - 1], "ctx", [(1, 0)])
    extended = jnp.concatenate([grad_conv, head_rows], axis=0)
    grad_convin = sum(
        conv_w_own[k] * extended[KCONV - 1 - k : KCONV - 1 - k + length] for k in range(KCONV)
    )
    grad_proj = jnp.concatenate([grad_gate.astype(BF), grad_convin.astype(BF)], axis=1)
    grad_rows_in = dot(grad_proj, w_main, 1, 1) + dot(grad_pre_low, w_dt_own, 1, 1)
    grad_normed = lax.psum_scatter(
        grad_rows_in.astype(BF), "tensor", scatter_dimension=0, tiled=True
    ).astype(F32)
    grad_wmain = dot(rows_all, grad_proj, 0, 0)
    grad_wdt = place(NH, dot(rows_all, grad_pre_low, 0, 0), head_start)
    unit = residual * inv_rms
    grad_unit = grad_normed * gain
    grad_gain = jnp.sum(grad_normed * unit, axis=0)
    grad_prev = grad_own + inv_rms * (
        grad_unit - unit * jnp.mean(grad_unit * unit, axis=-1, keepdims=True)
    )
    main = jnp.concatenate(
        [grad_wmain.astype(BF), grad_wdt.astype(BF), grad_wout_t.astype(BF)], axis=1
    )
    spread_chan = lambda g: jnp.concatenate(
        [place(INNER, g[..., :inner_loc], chan_start), g[..., inner_loc:]], axis=-1
    )
    small = (
        spread_chan(grad_convw),
        spread_chan(grad_convb),
        place(INNER, grad_normw, chan_start),
        grad_gain,
        place(NH, grad_dtbias, head_start),
        place(NH, grad_alog, head_start),
        place(NH, grad_skip, head_start),
    )
    return grad_prev, (main, small)


def per_device(*arrays):
    tokens, cotangent = arrays[0], arrays[-1]
    stack = arrays[1:-1]
    w_z, conv_w = stack[1], stack[5]
    tensor_at = lax.axis_index("tensor")
    ctx_at = lax.axis_index("ctx")
    groups = lax.axis_size("tensor")
    peers = lax.axis_size("dp") * lax.axis_size("ctx")
    inner_loc, heads_loc = INNER // groups, NH // groups
    residual = tokens[0].astype(F32)
    fetched = [fetch_layer(stack, layer) for layer in range(LAYERS)]
    kept = []
    for layer in range(LAYERS):
        residual, saved = layer_forward(residual, fetched[layer], tensor_at, inner_loc, heads_loc, ctx_at)
        kept.append(saved)
    result = residual.astype(BF)[None]
    grad = cotangent[0].astype(F32)
    reduced = [None] * LAYERS
    for layer in reversed(range(LAYERS)):
        grad, parts = layer_backward(
            grad, fetched[layer], kept[layer], tensor_at, inner_loc, heads_loc, ctx_at
        )
        reduced[layer] = reduce_layer(parts, peers)
    both = jnp.stack(reduced)
    rows = w_z.shape[1]
    at_bc, at_dt = 2 * inner_loc, 2 * inner_loc + 2 * NSTATE
    at_out = at_dt + NH
    shapes = [tuple(stack[i].shape[1:]) for i in (5, 6, 10, 0, 7, 8, 9)]
    sizes = []
    for shape in shapes:
        size = 1
        for extent in shape:
            size *= extent
        sizes.append(size)
    used = sum(sizes)
    mid = both[:, :rows, at_bc:at_out].reshape(LAYERS, -1)
    vec = both[:, rows:].reshape(LAYERS, -1)[:, :used]
    shared = lax.psum(jnp.concatenate([mid, vec], axis=1), "tensor").astype(F32)
    mid_sum = shared[:, : mid.shape[1]].reshape(LAYERS, rows, 2 * NSTATE + NH)
    pieces, at = [], mid.shape[1]
    for shape, size in zip(shapes, sizes):
        pieces.append(shared[:, at : at + size].reshape((LAYERS,) + shape))
        at += size
    g_convw, g_convb, g_normw, g_gain, g_dtb, g_alog, g_skip = pieces
    wide = both[:, :rows].astype(F32)
    return (
        result,
        grad[None],
        g_gain,
        wide[:, :, :inner_loc],
        wide[:, :, inner_loc : 2 * inner_loc],
        mid_sum[:, :, : 2 * NSTATE],
        mid_sum[:, :, 2 * NSTATE :],
        g_convw,
        g_convb,
        g_dtb,
        g_alog,
        g_skip,
        g_normw,
        jnp.swapaxes(wide[:, :, at_out:], 1, 2),
    )


def solution(mesh):
    placed = (
        P("dp", ("ctx", "tensor"), None),
        P(None, ("dp", "ctx")),
        P(None, ("dp", "ctx"), "tensor"),
        P(None, ("dp", "ctx"), "tensor"),
        P(None, ("dp", "ctx"), None),
        P(None, ("dp", "ctx"), None),
        P(None, None, ("dp", "ctx")),
        P(None, ("dp", "ctx")),
        P(None, ("dp", "ctx")),
        P(None, ("dp", "ctx")),
        P(None, ("dp", "ctx")),
        P(None, ("dp", "ctx")),
        P(None, "tensor", ("dp", "ctx")),
        P("dp", ("ctx", "tensor"), None),
    )
    return jax.shard_map(
        per_device,
        mesh=mesh,
        in_specs=placed,
        out_specs=(
            P("dp", ("ctx", "tensor"), None),
            P("dp", ("ctx", "tensor"), None),
            P(None, ("dp", "ctx")),
            P(None, ("dp", "ctx"), "tensor"),
            P(None, ("dp", "ctx"), "tensor"),
            P(None, ("dp", "ctx"), None),
            P(None, ("dp", "ctx"), None),
            P(None, None, ("dp", "ctx")),
            P(None, ("dp", "ctx")),
            P(None, ("dp", "ctx")),
            P(None, ("dp", "ctx")),
            P(None, ("dp", "ctx")),
            P(None, ("dp", "ctx")),
            P(None, "tensor", ("dp", "ctx")),
        ),
        check_vma=False,
    )
```
